256 devices in a mesh: fsdp: 64 (over z, y, core), tp: 4 (over x).
Axes of the slice: x: 4, y: 4, z: 8, core: 2. Of those that a mesh axis runs over, the one named last changes fastest.
Arguments:
- gradient: bfloat16 [8192, 22528], P('fsdp', 'tp'), may hold values from -6 to 6
- momentum: float32 [8192, 22528], P('fsdp', 'tp'), may hold values from -140 to 140, as said below
- weight: float32 [8192, 22528], P('fsdp', 'tp'), may hold values from -0.12 to 0.12
- basis: float32 [22528, 256], P(('tp', 'fsdp')), may hold values from -6 to 6
Outputs:
- new_momentum: float32 [8192, 22528], P('fsdp', 'tp')
- new_weight: float32 [8192, 22528], P('fsdp', 'tp')
- new_basis: float32 [22528, 256], P(('tp', 'fsdp'))
The draws below stay inside these ranges and needn't reach their ends.
Inputs may be any that keep to these rules, and one draw needn't show every extreme that they name: Real-valued momentum, rows and columns of differing scales.
All inputs are finite; a program needn't handle non-finite values.
Results may differ from the reference program's by a relative error of at most 0.0003.
Values sent between devices are 32-bit elements; how exact they have to be, the bound alone decides.
No kernel may reach another device: no remote copies, remote signals or barrier semaphores. Data moves between devices by JAX's collectives and lax.ppermute only.
A program may use at most 128 MiB of HBM per device.

```python
import math
import jax
import jax.numpy as jnp
from jax import lax

D = 8192
FF = 22528
RANK = 256


def draw_momentum(key, part):
    key = jax.random.fold_in(key, 7)
    first, second, third = jax.random.split(key, 3)
    values = jnp.clip(jax.random.normal(first, (D, FF), jnp.float32), -5.0, 5.0)
    spread = 10.0
    row_pos = jnp.arange(D, dtype=jnp.float32) / D
    col_pos = jnp.arange(FF, dtype=jnp.float32) / FF
    row_scale = jnp.exp(row_pos * math.log(3.0) + jax.random.uniform(second, (D,), jnp.float32) * math.log(spread))
    col_scale = jnp.exp(col_pos * math.log(3.0) + jax.random.uniform(third, (FF,), jnp.float32) * math.log(3.0))
    return (0.1 * values * row_scale[:, None] * col_scale[None, :]).astype(jnp.float32)


def level_of(key, dims, cuts, smallest, largest):
    gain, own = 1.0, jax.random.fold_in(key, 6)
    for dim, parts in cuts:
        steps = jnp.exp(jax.random.uniform(jax.random.fold_in(own, dim), (parts,), jnp.float32, smallest / len(cuts), largest / len(cuts)))
        gain = gain * jnp.repeat(steps, dims[dim] // parts).reshape([-1 if axis == dim else 1 for axis in range(len(dims))])
    return gain


def noise(stream_key, dims, width, limit, pieces=(), kind=jnp.bfloat16):
    level = level_of(stream_key, dims, pieces, -0.22, 0.18) if pieces else 1.0
    entries = jax.random.normal(stream_key, dims, jnp.float32) * width * level
    return jnp.minimum(jnp.maximum(entries, -limit), limit).astype(kind)


def setup_inputs(seed: int = 0) -> dict:
    key_list = jax.random.split(jax.random.key(seed), 5)
    gradient = noise(key_list[0], (D, FF), 1.0, 6.0, ((0, 64), (1, 4)))
    momentum = draw_momentum(jax.random.fold_in(key_list[4], 71), 0)
    weight = noise(key_list[2], (D, FF), 0.02, 0.12, ((0, 64), (1, 4)), jnp.float32)
    basis = noise(key_list[3], (FF, RANK), 1.0, 6.0, ((0, 256),), jnp.float32)
    return dict(gradient=gradient, momentum=momentum, weight=weight, basis=basis)


epsilon = 1e-06
feedback_keep = 0.05
step_rate = 0.1
weight_decay = 0.1

def reference(gradient, momentum, weight, basis):
    precise = lax.Precision.HIGHEST
    summed = momentum + gradient.astype(jnp.float32)
    projected = jnp.dot(summed.astype(jnp.float32), basis.astype(jnp.float32), precision=precise, preferred_element_type=jnp.float32)
    gram_matrix = jnp.dot(projected.T.astype(jnp.float32), projected.astype(jnp.float32), precision=precise, preferred_element_type=jnp.float32)
    factor = jnp.linalg.cholesky(gram_matrix)
    orthonormal = lax.linalg.triangular_solve(factor, projected, left_side=False, lower=True, transpose_a=True)
    feedback = jnp.dot(summed.T.astype(jnp.float32), orthonormal.astype(jnp.float32), precision=precise, preferred_element_type=jnp.float32)
    norms = jnp.sqrt(lax.optimization_barrier(jnp.sum(feedback * feedback, axis=0)))
    scales = math.sqrt(FF) / (norms + epsilon)
    new_basis = feedback * scales
    new_momentum = summed - feedback_keep * jnp.dot(orthonormal.astype(jnp.float32), feedback.T.astype(jnp.float32), precision=precise, preferred_element_type=jnp.float32)
    coeff_step = step_rate * math.sqrt(D / RANK) / math.sqrt(FF)
    new_weight = (1.0 - step_rate * weight_decay) * weight - coeff_step * jnp.dot(orthonormal.astype(jnp.float32), new_basis.T.astype(jnp.float32), precision=precise, preferred_element_type=jnp.float32)
    return (new_momentum, new_weight, new_basis)
```

```python
import math

import jax
import jax.numpy as jnp
from jax import lax
from jax.sharding import Mesh, PartitionSpec as P

D = 8192
FF = 22528
RANK = 256
NZ, NY, NC, NX = 8, 4, 2, 4


epsilon = 1e-06
feedback_keep = 0.05
step_rate = 0.1
weight_decay = 0.1


def dot(left, right, left_dim, right_dim, precision=lax.Precision.HIGH):
    return lax.dot_general(
        left,
        right,
        (((left_dim,), (right_dim,)), ((), ())),
        precision=precision,
        preferred_element_type=jnp.float32,
    )


def gather(block, axes, count):
    copies = jnp.broadcast_to(block[None], (count,) + block.shape)
    return lax.all_to_all(copies, axes, 0, 0)


def scatter_sum(blocks, axes):
    return jnp.sum(lax.all_to_all(blocks, axes, 0, 0), axis=0)


def swap(block):
    return lax.ppermute(block, "c", [(0, 1), (1, 0)])


def pair(mine, other, core, axis):
    return jnp.where(
        core == 0, jnp.stack([mine, other], axis), jnp.stack([other, mine], axis)
    )


def body(gradient, momentum, weight, basis):
    highest = lax.Precision.HIGHEST
    core, y, x = lax.axis_index("c"), lax.axis_index("y"), lax.axis_index("x")
    rows, cols = momentum.shape
    shard = basis.shape[0]
    summed = momentum + gradient.astype(jnp.float32)

    by_column = summed.T.reshape(NZ, NY, NC, shard, rows)
    by_column = jnp.moveaxis(by_column, 1, 0)
    by_column = lax.all_to_all(by_column, "y", 0, 0)
    strip = jnp.moveaxis(by_column.reshape(NY, NZ * NC * shard, rows), 0, 1)
    strip = strip.reshape(NZ * NC * shard, NY * rows)

    basis_z = gather(basis, "z", NZ)
    strip_basis = pair(basis_z, swap(basis_z), core, 1).reshape(NZ * NC * shard, RANK)

    partial_proj = dot(strip, strip_basis, 0, 0)
    few = rows // NX
    few_rows = scatter_sum(partial_proj.reshape(NY * NX, few, RANK), ("y", "x"))
    group_proj = gather(few_rows, ("y", "x"), NY * NX).reshape(NY * rows, RANK)
    projected = lax.dynamic_slice_in_dim(group_proj, y * rows, rows, 0)

    part = RANK // (NY * NX)
    gram_group = dot(group_proj, group_proj, 0, 0, highest)
    gram_part = lax.dynamic_slice_in_dim(gram_group, (y * NX + x) * part, part, 0)
    gram_part = gram_part + swap(gram_part)
    gram_part = jnp.sum(gather(gram_part, "z", NZ), axis=0)
    gram_matrix = gather(gram_part, ("y", "x"), NY * NX).reshape(RANK, RANK)
    factor = jnp.linalg.cholesky(gram_matrix)
    inverse = lax.linalg.triangular_solve(
        factor, jnp.eye(RANK, dtype=jnp.float32), left_side=True, lower=True
    )

    raw = dot(strip, group_proj, 1, 0).reshape(NZ, NC, shard, RANK)
    mine = lax.dynamic_index_in_dim(raw, core, 1, keepdims=False)
    other = lax.dynamic_index_in_dim(raw, 1 - core, 1, keepdims=False)
    raw_shard = scatter_sum(mine + swap(other), "z")
    raw_half = gather(raw_shard, ("z", "y"), NZ * NY)
    raw_full = pair(raw_half, swap(raw_half), core, 1).reshape(cols, RANK)

    orthonormal = dot(projected, inverse, 1, 1, highest)
    feedback = dot(raw_full, inverse, 1, 1)
    squares = jnp.sum(feedback * feedback, axis=0, keepdims=True)
    squares = squares + sum(
        lax.ppermute(squares, "x", [(i, (i + step) % NX) for i in range(NX)])
        for step in range(1, NX)
    )
    scales = math.sqrt(FF) / (jnp.sqrt(squares) + epsilon)
    coeff_step = step_rate * math.sqrt(D / RANK) / math.sqrt(FF)
    keep_weight = 1.0 - step_rate * weight_decay
    new_momentum = summed - feedback_keep * dot(orthonormal, feedback, 1, 1)
    new_weight = keep_weight * weight - coeff_step * dot(
        orthonormal * scales, feedback, 1, 1
    )
    new_basis = dot(raw_shard, inverse, 1, 1) * scales
    return (new_momentum, new_weight, new_basis)


def solution(mesh):
    fine = Mesh(mesh.devices.reshape(NZ, NY, NC, NX), ("z", "y", "c", "x"))
    matrix = P(("z", "y", "c"), "x")
    tall = P(("x", "z", "y", "c"), None)
    return jax.shard_map(
        body,
        mesh=fine,
        in_specs=(matrix, matrix, matrix, tall),
        out_specs=(matrix, matrix, tall),
        check_vma=False,
    )
```

```python
import math

import jax
import jax.numpy as jnp
from jax import lax
from jax.experimental import pallas as pl
from jax.experimental.pallas import tpu as pltpu
from jax.sharding import Mesh, PartitionSpec as P

D = 8192
FF = 22528
RANK = 256
NZ, NY, NC, NX = 8, 4, 2, 4


epsilon = 1e-06
feedback_keep = 0.05
step_rate = 0.1
weight_decay = 0.1

VMEM_BYTES = 50 * 1024 * 1024
HIGHEST = lax.Precision.HIGHEST


def dot(left, right, left_dim, right_dim, precision=lax.Precision.HIGH):
    return lax.dot_general(
        left,
        right,
        (((left_dim,), (right_dim,)), ((), ())),
        precision=precision,
        preferred_element_type=jnp.float32,
    )


def gather(block, axes, count):
    copies = jnp.broadcast_to(block[None], (count,) + block.shape)
    return lax.all_to_all(copies, axes, 0, 0)


def scatter_sum(blocks, axes):
    return jnp.sum(lax.all_to_all(blocks, axes, 0, 0), axis=0)


def swap(block):
    return lax.ppermute(block, "c", [(0, 1), (1, 0)])


def shift(block, axis, size, step):
    return lax.ppermute(block, axis, [(i, (i + step) % size) for i in range(size)])


def halves(value):
    high = value.astype(jnp.bfloat16)
    low = (value - high.astype(jnp.float32)).astype(jnp.bfloat16)
    return high, low


def dot_halves(left, right, left_dim, right_dim):
    def one(a, b):
        return lax.dot_general(
            a,
            b,
            (((left_dim,), (right_dim,)), ((), ())),
            preferred_element_type=jnp.float32,
        )

    (lh, ll), (rh, rl) = left, right
    return one(lh, rh) + (one(lh, rl) + one(ll, rh))


def params():
    return pltpu.CompilerParams(vmem_limit_bytes=VMEM_BYTES)


def cost(flops, size):
    return pl.CostEstimate(flops=flops, bytes_accessed=size, transcendentals=0)


def smem():
    return pl.BlockSpec(memory_space=pltpu.SMEM)


def split_kernel(pos, grad, mom, out0, out1, out2, out3, turned):
    y = pos[0]
    turned[...] = (mom[...] + grad[...].astype(jnp.float32)).T
    size = out0.shape[1]
    for d, out in enumerate((out0, out1, out2, out3)):
        owner = lax.rem(y + d, NY)
        for part in range(out.shape[0]):
            start = pl.multiple_of((part * NY + owner) * size, 8)
            out[part] = turned[pl.ds(start, size), :]


def split_columns(pos, gradient, momentum):
    rows, cols = momentum.shape
    wide = 2 * cols // NZ
    size = wide // (2 * NY)
    block = pl.BlockSpec((rows, wide), lambda i: (0, i))
    piece = pl.BlockSpec((2, size, rows), lambda i: (i, 0, 0))
    return pl.pallas_call(
        split_kernel,
        grid=(NZ // 2,),
        in_specs=[smem(), block, block],
        out_specs=[piece] * NY,
        out_shape=[jax.ShapeDtypeStruct((NZ, size, rows), jnp.float32)] * NY,
        scratch_shapes=[pltpu.VMEM((wide, rows), jnp.float32)],
        compiler_params=params(),
        cost_estimate=cost(0, rows * cols * 10),
    )(pos, gradient, momentum)


def project_kernel(pos, s0, s1, s2, s3, mine, other, out, full):
    y, core = pos[0], pos[1]
    half = mine.shape[1]
    for z in range(NZ):
        start = pl.multiple_of(z * 2 * half + core * half, 8)
        full[pl.ds(start, half), :] = mine[z]
        start = pl.multiple_of(z * 2 * half + (1 - core) * half, 8)
        full[pl.ds(start, half), :] = other[z]
    right = halves(full[...])
    for d, strip in enumerate((s0, s1, s2, s3)):
        left = halves(strip[...])
        out[lax.rem(y + NY - d, NY)] = dot_halves(left, right, 0, 0)


def project(pos, strips, mine, other):
    cols, rows = strips[0].shape
    return pl.pallas_call(
        project_kernel,
        in_specs=[smem()] + [pl.BlockSpec(memory_space=pltpu.VMEM)] * 6,
        out_specs=pl.BlockSpec(memory_space=pltpu.VMEM),
        out_shape=jax.ShapeDtypeStruct((NY, rows, RANK), jnp.float32),
        scratch_shapes=[pltpu.VMEM((cols, RANK), jnp.float32)],
        compiler_params=params(),
        cost_estimate=cost(6 * NY * rows * cols * RANK, NY * rows * cols * 8),
    )(pos, *strips, mine, other)


def feedback_kernel(pos, s0, s1, s2, s3, proj, gram, mine, other, low, high, full):
    y, core = pos[0], pos[1]
    rows = s0.shape[2]
    half = mine.shape[1] - gram.shape[0]

    @pl.when(pl.program_id(0) == 0)
    def _():
        for d in range(NY):
            top, rest = halves(proj[lax.rem(y + NY - d, NY)])
            high[d * rows : (d + 1) * rows] = top
            low[d * rows : (d + 1) * rows] = rest

    strip = jnp.concatenate([s0[0], s1[0], s2[0], s3[0]], axis=1)
    full[...] = dot_halves(halves(strip), (high[...], low[...]), 1, 0)
    mine[0, :half] = full[pl.ds(pl.multiple_of(core * half, 8), half), :]
    other[0, :half] = full[pl.ds(pl.multiple_of((1 - core) * half, 8), half), :]
    mine[0, half:] = gram[...]
    other[0, half:] = gram[...]


def raw_feedback(pos, strips, proj, gram):
    _, size, rows = strips[0].shape
    part = gram.shape[0]
    strip = pl.BlockSpec((1, size, rows), lambda z: (z, 0, 0))
    whole = lambda shape: pl.BlockSpec(shape, lambda z: (0,) * len(shape))
    out = pl.BlockSpec((1, size // 2 + part, RANK), lambda z: (z, 0, 0))
    return pl.pallas_call(
        feedback_kernel,
        grid=(NZ,),
        in_specs=[smem()] + [strip] * NY + [whole(proj.shape), whole(gram.shape)],
        out_specs=[out] * 2,
        out_shape=[jax.ShapeDtypeStruct((NZ, size // 2 + part, RANK), jnp.float32)] * 2,
        scratch_shapes=[
            pltpu.VMEM((NY * rows, RANK), jnp.bfloat16),
            pltpu.VMEM((NY * rows, RANK), jnp.bfloat16),
            pltpu.VMEM((size, RANK), jnp.float32),
        ],
        compiler_params=params(),
        cost_estimate=cost(6 * NY * rows * NZ * size * RANK, NZ * size * rows * 24),
    )(pos, *strips, proj, gram)


BLOCK = 64


def small_inverse(block):
    rows = lax.broadcasted_iota(jnp.int32, (BLOCK, BLOCK), 0)
    cols = lax.broadcasted_iota(jnp.int32, (BLOCK, BLOCK), 1)
    unit = (rows == cols).astype(jnp.float32)
    wide = jnp.concatenate([block, unit], axis=1)
    tiles = [wide[8 * t : 8 * t + 8] for t in range(BLOCK // 8)]
    place = lax.broadcasted_iota(jnp.int32, (8, 2 * BLOCK), 0)
    scale = [jnp.zeros((8, 2 * BLOCK), jnp.float32) for _ in tiles]
    for j in range(BLOCK):
        tile, row = divmod(j, 8)
        line = jnp.broadcast_to(tiles[tile][row : row + 1], (8, 2 * BLOCK))
        pivot = jnp.broadcast_to(line[:, j : j + 1], (8, 2 * BLOCK))
        line = line * (1.0 / pivot)
        scale[tile] = jnp.where(place == row, pivot, scale[tile])
        for t in range(tile, BLOCK // 8):
            factor = jnp.broadcast_to(tiles[t][:, j : j + 1], (8, 2 * BLOCK))
            if t == tile:
                factor = jnp.where(place > row, factor, 0.0)
            tiles[t] = tiles[t] - factor * line
    tiles = [t * (1.0 / jnp.sqrt(s)) for t, s in zip(tiles, scale)]
    return jnp.concatenate(tiles, axis=0)[:, BLOCK:]


def inverse_kernel(gram, out, work, lower):
    work[...] = gram[...]
    out[...] = jnp.zeros_like(out)
    count = RANK // BLOCK
    for k in range(count):
        at, end = k * BLOCK, (k + 1) * BLOCK
        small = small_inverse(work[at:end, at:end])
        if k + 1 < count:
            panel = dot(work[end:, at:end], small, 1, 1, HIGHEST)
            lower[end:, at:end] = panel
            work[end:, end:] = work[end:, end:] - dot(panel, panel, 1, 1, HIGHEST)
        if k:
            above = dot(lower[at:end, :at], out[:at, :at], 1, 0, HIGHEST)
            out[at:end, :at] = -dot(small, above, 1, 0, HIGHEST)
        out[at:end, at:end] = small


def factor_inverse(gram):
    return pl.pallas_call(
        inverse_kernel,
        in_specs=[pl.BlockSpec(memory_space=pltpu.VMEM)],
        out_specs=pl.BlockSpec(memory_space=pltpu.VMEM),
        out_shape=jax.ShapeDtypeStruct((RANK, RANK), jnp.float32),
        scratch_shapes=[pltpu.VMEM((RANK, RANK), jnp.float32)] * 2,
        compiler_params=params(),
        cost_estimate=cost(10_000_000_000, 1_000_000),
    )(gram)


def update_kernel(pos, left, grad, mom, wgt, *refs):
    mine, other = refs[0:5], refs[5:10]
    new_mom, new_wgt, full = refs[10:]
    y, core, i = pos[0], pos[1], pl.program_id(0)
    half = mine[0].shape[1]

    def place(ref, d, first):
        owner = lax.rem(y + NY - d, NY)
        for part in range(2):
            start = ((part * NY + owner) * 2 + first) * half
            full[pl.ds(pl.multiple_of(start, 8), half), :] = ref[part]

    for group, first in ((mine, core), (other, 1 - core)):
        place(group[0], 0, first)
        place(group[1], 1, first)
        place(group[2], 3, first)

        @pl.when(i < 2)
        def _():
            place(group[3], 2, first)

        @pl.when(i >= 2)
        def _():
            place(group[4], 2, first)

    rows = mom.shape[0]
    both = dot_halves(halves(left[...]), halves(full[...]), 1, 1)
    coeff = step_rate * math.sqrt(D / RANK) / math.sqrt(FF)
    keep = 1.0 - step_rate * weight_decay
    summed = mom[...] + grad[...].astype(jnp.float32)
    new_mom[...] = summed - feedback_keep * both[:rows]
    new_wgt[...] = keep * wgt[...] - coeff * both[rows:]


def update(pos, left, gradient, momentum, weight, mine, other):
    rows, cols = momentum.shape
    wide = 2 * cols // NZ
    half = mine[0].shape[1]
    block = pl.BlockSpec((rows, wide), lambda i: (0, i))
    piece = pl.BlockSpec((2, half, RANK), lambda i: (i, 0, 0))
    early = pl.BlockSpec((2, half, RANK), lambda i: (jnp.minimum(i, 1), 0, 0))
    late = pl.BlockSpec((2, half, RANK), lambda i: (jnp.maximum(i - 2, 0), 0, 0))
    pieces = [piece] * 3 + [early, late]
    whole = pl.BlockSpec(left.shape, lambda i: (0, 0))
    return pl.pallas_call(
        update_kernel,
        grid=(NZ // 2,),
        in_specs=[smem(), whole, block, block, block] + pieces + pieces,
        out_specs=[block, block],
        out_shape=[jax.ShapeDtypeStruct(momentum.shape, jnp.float32)] * 2,
        scratch_shapes=[pltpu.VMEM((wide, RANK), jnp.float32)],
        compiler_params=params(),
        cost_estimate=cost(12 * rows * cols * RANK, rows * cols * 18),
    )(pos, left, gradient, momentum, weight, *mine, *other)


def body(gradient, momentum, weight, basis):
    core, y, x = lax.axis_index("c"), lax.axis_index("y"), lax.axis_index("x")
    pos = jnp.stack([y, core]).astype(jnp.int32)
    rows, cols = momentum.shape
    shard = basis.shape[0]

    basis_z = gather(basis, "z", NZ)

    sent = split_columns(pos, gradient, momentum)
    strips = [sent[0]] + [shift(sent[d], "y", NY, d) for d in range(1, NY)]
    flat = [strip.reshape(NZ * NC * shard, rows) for strip in strips]

    partial_proj = project(pos, flat, basis_z, swap(basis_z))
    few = rows // NX
    few_rows = scatter_sum(partial_proj.reshape(NY * NX, few, RANK), ("y", "x"))
    group_proj = gather(few_rows, ("y", "x"), NY * NX).reshape(NY, rows, RANK)
    projected = lax.dynamic_index_in_dim(group_proj, y, 0, keepdims=False)

    part = RANK // (NY * NX)
    all_rows = group_proj.reshape(NY * rows, RANK)
    gram_group = dot(all_rows, all_rows, 0, 0, HIGHEST)
    gram_part = lax.dynamic_slice_in_dim(gram_group, (y * NX + x) * part, part, 0)

    mine, other = raw_feedback(pos, strips, group_proj, gram_part)
    reduced = scatter_sum(mine + swap(other), "z")
    raw_shard, gram_part = reduced[:shard], reduced[shard:]

    raw = gather(raw_shard, "z", NZ)
    ahead = shift(raw, "y", NY, 1)
    behind = shift(raw, "y", NY, NY - 1)
    ahead2 = shift(ahead[: NZ // 2], "y", NY, 1)
    behind2 = shift(behind[NZ // 2 :], "y", NY, NY - 1)
    own = [raw, ahead, behind, ahead2, behind2]
    paired = [swap(block) for block in own]

    by_y = jnp.stack([gram_part] + [shift(gram_part, "y", NY, d) for d in range(1, NY)])
    by_x = jnp.stack([by_y] + [shift(by_y, "x", NX, d) for d in range(1, NX)])
    by_x = jnp.flip(jnp.concatenate([by_x, by_x], 0), 0)
    by_x = lax.dynamic_slice_in_dim(by_x, NX - 1 - x, NX, 0)
    by_y = jnp.flip(jnp.concatenate([by_x, by_x], 1), 1)
    by_y = lax.dynamic_slice_in_dim(by_y, NY - 1 - y, NY, 1)
    gram_matrix = jnp.swapaxes(by_y, 0, 1).reshape(RANK, RANK)
    inverse = factor_inverse(gram_matrix)

    orthonormal = dot(projected, inverse, 1, 1, HIGHEST)
    strip_feedback = dot(raw.reshape(NZ * shard, RANK), inverse, 1, 1)
    squares = jnp.sum(strip_feedback * strip_feedback, axis=0, keepdims=True)
    squares = squares + swap(squares)
    squares = jnp.sum(gather(squares, ("y", "x"), NY * NX), axis=0)
    scales = math.sqrt(FF) / (jnp.sqrt(squares) + epsilon)

    left = jnp.concatenate([orthonormal, orthonormal * scales], axis=0)
    left = dot(left, inverse, 1, 0, HIGHEST)
    new_momentum, new_weight = update(
        pos, left, gradient, momentum, weight, own, paired
    )
    new_basis = dot(raw_shard, inverse, 1, 1) * scales
    return (new_momentum, new_weight, new_basis)


def solution(mesh):
    fine = Mesh(mesh.devices.reshape(NZ, NY, NC, NX), ("z", "y", "c", "x"))
    matrix = P(("z", "y", "c"), "x")
    tall = P(("x", "z", "y", "c"), None)
    return jax.shard_map(
        body,
        mesh=fine,
        in_specs=(matrix, matrix, matrix, tall),
        out_specs=(matrix, matrix, tall),
        check_vma=False,
    )
```

```python
import functools
import math

import jax
import jax.numpy as jnp
from jax import lax
from jax.experimental import pallas as pl
from jax.experimental.pallas import tpu as pltpu
from jax.sharding import Mesh, PartitionSpec as P

D = 8192
FF = 22528
RANK = 256
NZ, NY, NC, NX = 8, 4, 2, 4


epsilon = 1e-06
feedback_keep = 0.05
step_rate = 0.1
weight_decay = 0.1

MIB = 1024 * 1024
HIGHEST = lax.Precision.HIGHEST


def dot(left, right, left_dim, right_dim, precision=lax.Precision.HIGH):
    return lax.dot_general(
        left,
        right,
        (((left_dim,), (right_dim,)), ((), ())),
        precision=precision,
        preferred_element_type=jnp.float32,
    )


def gather(block, axes, count):
    copies = jnp.broadcast_to(block[None], (count,) + block.shape)
    return lax.all_to_all(copies, axes, 0, 0)


def scatter_sum(blocks, axes):
    return jnp.sum(lax.all_to_all(blocks, axes, 0, 0), axis=0)


def swap(block):
    return lax.ppermute(block, "c", [(0, 1), (1, 0)])


def shift(block, axis, size, step):
    return lax.ppermute(block, axis, [(i, (i + step) % size) for i in range(size)])


def halves(value):
    high = value.astype(jnp.bfloat16)
    low = (value - high.astype(jnp.float32)).astype(jnp.bfloat16)
    return high, low


def dot_halves(left, right, left_dim, right_dim):
    def one(a, b):
        return lax.dot_general(
            a,
            b,
            (((left_dim,), (right_dim,)), ((), ())),
            preferred_element_type=jnp.float32,
        )

    (lh, ll), (rh, rl) = left, right
    return one(lh, rh) + (one(lh, rl) + one(ll, rh))


def params(mib):
    return pltpu.CompilerParams(vmem_limit_bytes=mib * MIB)


def cost(flops, size):
    return pl.CostEstimate(flops=flops, bytes_accessed=size, transcendentals=0)


def smem():
    return pl.BlockSpec(memory_space=pltpu.SMEM)


def split_kernel(pos, grad, mom, out0, out1, out2, out3, turned):
    y = pos[0]
    turned[...] = (mom[...] + grad[...].astype(jnp.float32)).T
    size = out0.shape[1]
    for d, out in enumerate((out0, out1, out2, out3)):
        owner = lax.rem(y + d, NY)
        for part in range(out.shape[0]):
            start = pl.multiple_of((part * NY + owner) * size, 8)
            out[part] = turned[pl.ds(start, size), :]


def split_columns(pos, gradient, momentum):
    rows, cols = momentum.shape
    wide = 2 * cols // NZ
    size = wide // (2 * NY)
    block = pl.BlockSpec((rows, wide), lambda i: (0, i))
    piece = pl.BlockSpec((2, size, rows), lambda i: (i, 0, 0))
    return pl.pallas_call(
        split_kernel,
        grid=(NZ // 2,),
        in_specs=[smem(), block, block],
        out_specs=[piece] * NY,
        out_shape=[jax.ShapeDtypeStruct((NZ, size, rows), jnp.float32)] * NY,
        scratch_shapes=[pltpu.VMEM((wide, rows), jnp.float32)],
        compiler_params=params(16),
        cost_estimate=cost(0, rows * cols * 10),
    )(pos, gradient, momentum)


def project_kernel(count, pos, *refs):
    core = pos[1]
    mine, other = refs[count : count + 2]
    full = refs[-1]
    half = mine.shape[1]
    for z in range(NZ):
        start = pl.multiple_of(z * 2 * half + core * half, 8)
        full[pl.ds(start, half), :] = mine[z]
        start = pl.multiple_of(z * 2 * half + (1 - core) * half, 8)
        full[pl.ds(start, half), :] = other[z]
    right = halves(full[...])
    for strip, out in zip(refs[:count], refs[count + 2 : -1]):
        out[...] = dot_halves(halves(strip[...]), right, 0, 0)


def project(pos, strips, mine, other):
    cols, rows = strips[0].shape
    count = len(strips)
    return pl.pallas_call(
        functools.partial(project_kernel, count),
        in_specs=[smem()] + [pl.BlockSpec(memory_space=pltpu.VMEM)] * (count + 2),
        out_specs=[pl.BlockSpec(memory_space=pltpu.VMEM)] * count,
        out_shape=[jax.ShapeDtypeStruct((rows, RANK), jnp.float32)] * count,
        scratch_shapes=[pltpu.VMEM((cols, RANK), jnp.float32)],
        compiler_params=params(24),
        cost_estimate=cost(6 * count * rows * cols * RANK, count * rows * cols * 8),
    )(pos, *strips, mine, other)


def feedback_kernel(pos, s0, s1, s2, s3, p0, p1, p2, p3, mine, other, low, high, full, gram):
    core = pos[1]
    rows = s0.shape[2]
    steps, size = s0.shape[:2]
    half = size // 2
    part = mine.shape[1] - half

    @pl.when(pl.program_id(0) == 0)
    def _():
        proj = jnp.concatenate([p0[...], p1[...], p2[...], p3[...]], axis=0)
        high[...], low[...] = halves(proj)
        gram[...] = dot(proj, proj, 0, 0, HIGHEST)

    mine_at = pl.multiple_of(core * half, 8)
    other_at = pl.multiple_of((1 - core) * half, 8)
    gram_rows = gram[pl.ds(pl.multiple_of(pos[2] * part, 8), part), :]
    for z in range(steps):
        strip = jnp.concatenate([s0[z], s1[z], s2[z], s3[z]], axis=1)
        full[...] = dot_halves(halves(strip), (high[...], low[...]), 1, 0)
        mine[z, :half] = full[pl.ds(mine_at, half), :]
        other[z, :half] = full[pl.ds(other_at, half), :]
        mine[z, half:] = gram_rows
        other[z, half:] = gram_rows


def raw_feedback(pos, strips, projs):
    _, size, rows = strips[0].shape
    part = RANK // (NY * NX)
    steps = 2
    strip = pl.BlockSpec((steps, size, rows), lambda z: (z, 0, 0))
    proj = pl.BlockSpec((rows, RANK), lambda z: (0, 0))
    out = pl.BlockSpec((steps, size // 2 + part, RANK), lambda z: (z, 0, 0))
    return pl.pallas_call(
        feedback_kernel,
        grid=(NZ // steps,),
        in_specs=[smem()] + [strip] * NY + [proj] * NY,
        out_specs=[out] * 2,
        out_shape=[jax.ShapeDtypeStruct((NZ, size // 2 + part, RANK), jnp.float32)] * 2,
        scratch_shapes=[
            pltpu.VMEM((NY * rows, RANK), jnp.bfloat16),
            pltpu.VMEM((NY * rows, RANK), jnp.bfloat16),
            pltpu.VMEM((size, RANK), jnp.float32),
            pltpu.VMEM((RANK, RANK), jnp.float32),
        ],
        compiler_params=params(24),
        cost_estimate=cost(6 * NY * rows * NZ * size * RANK, NZ * size * rows * 24),
    )(pos, *strips, *projs)


BLOCK = 64
GROUP = 8


def small_inverse(block):
    rows = lax.broadcasted_iota(jnp.int32, (BLOCK, BLOCK), 0)
    cols = lax.broadcasted_iota(jnp.int32, (BLOCK, BLOCK), 1)
    unit = (rows == cols).astype(jnp.float32)
    wide = jnp.concatenate([block, unit], axis=1)
    full = (8, 2 * BLOCK)
    tiles = [wide[8 * t : 8 * t + 8] for t in range(BLOCK // 8)]
    place = lax.broadcasted_iota(jnp.int32, full, 0)
    scale = [jnp.zeros(full, jnp.float32) for _ in tiles]
    for j in range(0, BLOCK, GROUP):
        tile, row = divmod(j, 8)
        cols = {
            t: [jnp.broadcast_to(tiles[t][:, j + k : j + k + 1], full) for k in range(GROUP)]
            for t in range(tile, BLOCK // 8)
        }
        lines = [
            jnp.broadcast_to(tiles[tile][row + k : row + k + 1], full) for k in range(GROUP)
        ]
        heads = [
            [
                jnp.broadcast_to(cols[tile][m][row + k : row + k + 1], full)
                for m in range(k + 1)
            ]
            for k in range(GROUP)
        ]
        pivots = []
        for m in range(GROUP):
            pivot = heads[m][m]
            inverse = 1.0 / pivot
            pivots.append((pivot, inverse))
            for k in range(m + 1, GROUP):
                ratio = heads[k][m] * inverse
                lines[k] = lines[k] - ratio * lines[m]
                for n in range(m + 1, k + 1):
                    heads[k][n] = heads[k][n] - ratio * heads[n][m]
                for t in cols:
                    cols[t][k] = cols[t][k] - ratio * cols[t][m]
        scaled = [line * inverse for line, (_, inverse) in zip(lines, pivots)]
        for t in cols:
            change = cols[t][0] * scaled[0]
            for k in range(1, GROUP):
                change = change + cols[t][k] * scaled[k]
            if t == tile:
                change = jnp.where(place >= row + GROUP, change, 0.0)
                kept = tiles[t] - change
                for k in range(GROUP):
                    kept = jnp.where(place == row + k, lines[k], kept)
                    scale[t] = jnp.where(place == row + k, pivots[k][0], scale[t])
                tiles[t] = kept
            else:
                tiles[t] = tiles[t] - change
    tiles = [t * (1.0 / jnp.sqrt(s)) for t, s in zip(tiles, scale)]
    return jnp.concatenate(tiles, axis=0)[:, BLOCK:]


def inverse_kernel(gram, out, work, lower):
    work[...] = gram[...]
    out[...] = jnp.zeros_like(out)
    count = RANK // BLOCK
    for k in range(count):
        at, end = k * BLOCK, (k + 1) * BLOCK
        small = small_inverse(work[at:end, at:end])
        if k + 1 < count:
            panel = dot(work[end:, at:end], small, 1, 1, HIGHEST)
            lower[end:, at:end] = panel
            work[end:, end:] = work[end:, end:] - dot(panel, panel, 1, 1, HIGHEST)
        if k:
            above = dot(lower[at:end, :at], out[:at, :at], 1, 0, HIGHEST)
            out[at:end, :at] = -dot(small, above, 1, 0, HIGHEST)
        out[at:end, at:end] = small


def factor_inverse(gram):
    return pl.pallas_call(
        inverse_kernel,
        in_specs=[pl.BlockSpec(memory_space=pltpu.VMEM)],
        out_specs=pl.BlockSpec(memory_space=pltpu.VMEM),
        out_shape=jax.ShapeDtypeStruct((RANK, RANK), jnp.float32),
        scratch_shapes=[pltpu.VMEM((RANK, RANK), jnp.float32)] * 2,
        compiler_params=params(16),
        cost_estimate=cost(10_000_000_000, 1_000_000),
    )(gram)


def update_kernel(pos, left, grad, mom, wgt, *refs):
    mine, other = refs[0:5], refs[5:10]
    new_mom, new_wgt, full = refs[10:]
    y, core, i = pos[0], pos[1], pl.program_id(0)
    half = mine[0].shape[1]

    def place(ref, d, first):
        owner = lax.rem(y + NY - d, NY)
        for part in range(2):
            start = ((part * NY + owner) * 2 + first) * half
            full[pl.ds(pl.multiple_of(start, 8), half), :] = ref[part]

    for group, first in ((mine, core), (other, 1 - core)):
        place(group[0], 0, first)
        place(group[1], 1, first)
        place(group[2], 3, first)

        @pl.when(i < 2)
        def _():
            place(group[3], 2, first)

        @pl.when(i >= 2)
        def _():
            place(group[4], 2, first)

    rows = mom.shape[0]
    both = dot_halves(halves(left[...]), halves(full[...]), 1, 1)
    coeff = step_rate * math.sqrt(D / RANK) / math.sqrt(FF)
    keep = 1.0 - step_rate * weight_decay
    summed = mom[...] + grad[...].astype(jnp.float32)
    new_mom[...] = summed - feedback_keep * both[:rows]
    new_wgt[...] = keep * wgt[...] - coeff * both[rows:]


def update(pos, left, gradient, momentum, weight, mine, other):
    rows, cols = momentum.shape
    wide = 2 * cols // NZ
    half = mine[0].shape[1]
    block = pl.BlockSpec((rows, wide), lambda i: (0, i))
    piece = pl.BlockSpec((2, half, RANK), lambda i: (i, 0, 0))
    early = pl.BlockSpec((2, half, RANK), lambda i: (jnp.minimum(i, 1), 0, 0))
    late = pl.BlockSpec((2, half, RANK), lambda i: (jnp.maximum(i - 2, 0), 0, 0))
    pieces = [piece] * 3 + [early, late]
    whole = pl.BlockSpec(left.shape, lambda i: (0, 0))
    return pl.pallas_call(
        update_kernel,
        grid=(NZ // 2,),
        in_specs=[smem(), whole, block, block, block] + pieces + pieces,
        out_specs=[block, block],
        out_shape=[jax.ShapeDtypeStruct(momentum.shape, jnp.float32)] * 2,
        scratch_shapes=[pltpu.VMEM((wide, RANK), jnp.float32)],
        compiler_params=params(28),
        cost_estimate=cost(12 * rows * cols * RANK, rows * cols * 18),
    )(pos, left, gradient, momentum, weight, *mine, *other)


def body(gradient, momentum, weight, basis):
    core, y, x = lax.axis_index("c"), lax.axis_index("y"), lax.axis_index("x")
    pos = jnp.stack([y, core, y * NX + x]).astype(jnp.int32)
    rows, cols = momentum.shape
    shard = basis.shape[0]

    sent = split_columns(pos, gradient, momentum)
    sent, basis = lax.optimization_barrier((sent, basis))
    strips = [sent[0], None, None, None]
    for d in (2, 1, 3):
        strips[d] = shift(sent[d], "y", NY, d)
    flat = [strip.reshape(NZ * NC * shard, rows) for strip in strips]

    basis_z = gather(basis, "z", NZ)
    basis_other = swap(basis_z)
    near, first, third = project(pos, [flat[0], flat[1], flat[3]], basis_z, basis_other)
    (second,) = project(pos, [flat[2]], basis_z, basis_other)
    projected = (
        near
        + shift(first, "y", NY, NY - 1)
        + shift(third, "y", NY, 1)
        + shift(second, "y", NY, 2)
    )
    projected = projected + sum(shift(projected, "x", NX, d) for d in range(1, NX))
    projs = [projected] + [shift(projected, "y", NY, d) for d in range(1, NY)]

    mine, other = raw_feedback(pos, strips, projs)
    reduced = scatter_sum(mine + swap(other), "z")
    raw_shard, gram_part = reduced[:shard], reduced[shard:]

    raw = gather(raw_shard, "z", NZ)
    by_y = jnp.stack([gram_part] + [shift(gram_part, "y", NY, d) for d in range(1, NY)])
    by_x = jnp.stack([by_y] + [shift(by_y, "x", NX, d) for d in range(1, NX)])
    by_x = jnp.flip(jnp.concatenate([by_x, by_x], 0), 0)
    by_x = lax.dynamic_slice_in_dim(by_x, NX - 1 - x, NX, 0)
    by_y = jnp.flip(jnp.concatenate([by_x, by_x], 1), 1)
    by_y = lax.dynamic_slice_in_dim(by_y, NY - 1 - y, NY, 1)
    gram_matrix = jnp.swapaxes(by_y, 0, 1).reshape(RANK, RANK)
    inverse = factor_inverse(gram_matrix)

    raw, inverse = lax.optimization_barrier((raw, inverse))
    ahead = shift(raw, "y", NY, 1)
    behind = shift(raw, "y", NY, NY - 1)
    ahead2 = shift(ahead[: NZ // 2], "y", NY, 1)
    behind2 = shift(behind[NZ // 2 :], "y", NY, NY - 1)
    own = [raw, ahead, behind, ahead2, behind2]
    paired = [swap(block) for block in own]

    orthonormal = dot(projected, inverse, 1, 1, HIGHEST)
    strip_feedback = dot(raw.reshape(NZ * shard, RANK), inverse, 1, 1)
    squares = jnp.sum(strip_feedback * strip_feedback, axis=0, keepdims=True)
    squares = squares + swap(squares)
    squares = jnp.sum(gather(squares, ("y", "x"), NY * NX), axis=0)
    scales = math.sqrt(FF) / (jnp.sqrt(squares) + epsilon)

    left = jnp.concatenate([orthonormal, orthonormal * scales], axis=0)
    left = dot(left, inverse, 1, 0, HIGHEST)
    new_momentum, new_weight = update(
        pos, left, gradient, momentum, weight, own, paired
    )
    new_basis = dot(raw_shard, inverse, 1, 1) * scales
    return (new_momentum, new_weight, new_basis)


def solution(mesh):
    fine = Mesh(mesh.devices.reshape(NZ, NY, NC, NX), ("z", "y", "c", "x"))
    matrix = P(("z", "y", "c"), "x")
    tall = P(("x", "z", "y", "c"), None)
    return jax.shard_map(
        body,
        mesh=fine,
        in_specs=(matrix, matrix, matrix, tall),
        out_specs=(matrix, matrix, tall),
        check_vma=False,
    )
```

```python
import functools
import math

import jax
import jax.numpy as jnp
from jax import lax
from jax.experimental import pallas as pl
from jax.experimental.pallas import tpu as pltpu
from jax.sharding import Mesh, PartitionSpec as P

D = 8192
FF = 22528
RANK = 256
NZ, NY, NC, NX = 8, 4, 2, 4


epsilon = 1e-06
feedback_keep = 0.05
step_rate = 0.1
weight_decay = 0.1

MIB = 1024 * 1024
HIGHEST = lax.Precision.HIGHEST


def dot(left, right, left_dim, right_dim, precision=lax.Precision.HIGH):
    return lax.dot_general(
        left,
        right,
        (((left_dim,), (right_dim,)), ((), ())),
        precision=precision,
        preferred_element_type=jnp.float32,
    )


def gather(block, axes, count):
    copies = jnp.broadcast_to(block[None], (count,) + block.shape)
    return lax.all_to_all(copies, axes, 0, 0)


def scatter_sum(blocks, axes):
    return jnp.sum(lax.all_to_all(blocks, axes, 0, 0), axis=0)


def swap(block):
    return lax.ppermute(block, "c", [(0, 1), (1, 0)])


def shift(block, axis, size, step):
    return lax.ppermute(block, axis, [(i, (i + step) % size) for i in range(size)])


def halves(value):
    high = value.astype(jnp.bfloat16)
    low = (value - high.astype(jnp.float32)).astype(jnp.bfloat16)
    return high, low


def dot_halves(left, right, left_dim, right_dim):
    def one(a, b):
        return lax.dot_general(
            a,
            b,
            (((left_dim,), (right_dim,)), ((), ())),
            preferred_element_type=jnp.float32,
        )

    (lh, ll), (rh, rl) = left, right
    return one(lh, rh) + (one(lh, rl) + one(ll, rh))


def params(mib):
    return pltpu.CompilerParams(vmem_limit_bytes=mib * MIB)


def cost(flops, size):
    return pl.CostEstimate(flops=flops, bytes_accessed=size, transcendentals=0)


def smem():
    return pl.BlockSpec(memory_space=pltpu.SMEM)


def split_kernel(grad, mom, out, turned):
    turned[...] = (mom[...] + grad[...].astype(jnp.float32)).T
    size = out.shape[2]
    for part in range(out.shape[1]):
        for owner in range(NY):
            start = (part * NY + owner) * size
            out[owner, part] = turned[start : start + size]


def split_columns(gradient, momentum):
    rows, cols = momentum.shape
    wide = 2 * cols // NZ
    size = wide // (2 * NY)
    block = pl.BlockSpec((rows, wide), lambda i: (0, i))
    return pl.pallas_call(
        split_kernel,
        grid=(NZ // 2,),
        in_specs=[block, block],
        out_specs=pl.BlockSpec((NY, 2, size, rows), lambda i: (0, i, 0, 0)),
        out_shape=jax.ShapeDtypeStruct((NY, NZ, size, rows), jnp.float32),
        scratch_shapes=[pltpu.VMEM((wide, rows), jnp.float32)],
        compiler_params=params(60),
        cost_estimate=cost(0, rows * cols * 10),
    )(gradient, momentum)


def project_kernel(pos, strips, mine, other, o0, o1, o2, o3, full):
    y, core = pos[0], pos[1]
    half = mine.shape[1]
    for z in range(NZ):
        start = pl.multiple_of(z * 2 * half + core * half, 8)
        full[pl.ds(start, half), :] = mine[z]
        start = pl.multiple_of(z * 2 * half + (1 - core) * half, 8)
        full[pl.ds(start, half), :] = other[z]
    right = halves(full[...])
    for d, out in enumerate((o0, o1, o2, o3)):
        out[...] = dot_halves(halves(strips[lax.rem(y + NY - d, NY)]), right, 0, 0)


def project(pos, strips, mine, other):
    _, cols, rows = strips.shape
    return pl.pallas_call(
        project_kernel,
        in_specs=[smem()] + [pl.BlockSpec(memory_space=pltpu.VMEM)] * 3,
        out_specs=[pl.BlockSpec(memory_space=pltpu.VMEM)] * NY,
        out_shape=[jax.ShapeDtypeStruct((rows, RANK), jnp.float32)] * NY,
        scratch_shapes=[pltpu.VMEM((cols, RANK), jnp.float32)],
        compiler_params=params(24),
        cost_estimate=cost(6 * NY * rows * cols * RANK, NY * rows * cols * 8),
    )(pos, strips, mine, other)


def feedback_kernel(pos, strips, p0, p1, p2, p3, mine, other, low, high, full, gram):
    y, core = pos[0], pos[1]
    steps, size = strips.shape[1:3]
    half = size // 2
    part = mine.shape[1] - half

    @pl.when(pl.program_id(0) == 0)
    def _():
        proj = jnp.concatenate([p0[...], p1[...], p2[...], p3[...]], axis=0)
        high[...], low[...] = halves(proj)
        gram[...] = dot(proj, proj, 0, 0, HIGHEST)

    mine_at = pl.multiple_of(core * half, 8)
    other_at = pl.multiple_of((1 - core) * half, 8)
    gram_rows = gram[pl.ds(pl.multiple_of(pos[2] * part, 8), part), :]
    for z in range(steps):
        strip = jnp.concatenate(
            [strips[lax.rem(y + NY - d, NY), z] for d in range(NY)], axis=1
        )
        full[...] = dot_halves(halves(strip), (high[...], low[...]), 1, 0)
        mine[z, :half] = full[pl.ds(mine_at, half), :]
        other[z, :half] = full[pl.ds(other_at, half), :]
        mine[z, half:] = gram_rows
        other[z, half:] = gram_rows


def raw_feedback(pos, strips, projs):
    _, _, size, rows = strips.shape
    part = RANK // (NY * NX)
    steps = 2
    strip = pl.BlockSpec((NY, steps, size, rows), lambda z: (0, z, 0, 0))
    proj = pl.BlockSpec((rows, RANK), lambda z: (0, 0))
    out = pl.BlockSpec((steps, size // 2 + part, RANK), lambda z: (z, 0, 0))
    return pl.pallas_call(
        feedback_kernel,
        grid=(NZ // steps,),
        in_specs=[smem(), strip] + [proj] * NY,
        out_specs=[out] * 2,
        out_shape=[jax.ShapeDtypeStruct((NZ, size // 2 + part, RANK), jnp.float32)] * 2,
        scratch_shapes=[
            pltpu.VMEM((NY * rows, RANK), jnp.bfloat16),
            pltpu.VMEM((NY * rows, RANK), jnp.bfloat16),
            pltpu.VMEM((size, RANK), jnp.float32),
            pltpu.VMEM((RANK, RANK), jnp.float32),
        ],
        compiler_params=params(24),
        cost_estimate=cost(6 * NY * rows * NZ * size * RANK, NZ * size * rows * 24),
    )(pos, strips, *projs)


BLOCK = 64
GROUP = 8


def small_inverse(block):
    rows = lax.broadcasted_iota(jnp.int32, (BLOCK, BLOCK), 0)
    cols = lax.broadcasted_iota(jnp.int32, (BLOCK, BLOCK), 1)
    unit = (rows == cols).astype(jnp.float32)
    wide = jnp.concatenate([block, unit], axis=1)
    full = (8, 2 * BLOCK)
    tiles = [wide[8 * t : 8 * t + 8] for t in range(BLOCK // 8)]
    place = lax.broadcasted_iota(jnp.int32, full, 0)
    scale = [jnp.zeros(full, jnp.float32) for _ in tiles]
    for j in range(0, BLOCK, GROUP):
        tile, row = divmod(j, 8)
        cols = {
            t: [jnp.broadcast_to(tiles[t][:, j + k : j + k + 1], full) for k in range(GROUP)]
            for t in range(tile, BLOCK // 8)
        }
        lines = [
            jnp.broadcast_to(tiles[tile][row + k : row + k + 1], full) for k in range(GROUP)
        ]
        heads = [
            [
                jnp.broadcast_to(cols[tile][m][row + k : row + k + 1], full)
                for m in range(k + 1)
            ]
            for k in range(GROUP)
        ]
        pivots = []
        for m in range(GROUP):
            pivot = heads[m][m]
            inverse = 1.0 / pivot
            pivots.append((pivot, inverse))
            for k in range(m + 1, GROUP):
                ratio = heads[k][m] * inverse
                lines[k] = lines[k] - ratio * lines[m]
                for n in range(m + 1, k + 1):
                    heads[k][n] = heads[k][n] - ratio * heads[n][m]
                for t in cols:
                    cols[t][k] = cols[t][k] - ratio * cols[t][m]
        scaled = [line * inverse for line, (_, inverse) in zip(lines, pivots)]
        for t in cols:
            change = cols[t][0] * scaled[0]
            for k in range(1, GROUP):
                change = change + cols[t][k] * scaled[k]
            if t == tile:
                change = jnp.where(place >= row + GROUP, change, 0.0)
                kept = tiles[t] - change
                for k in range(GROUP):
                    kept = jnp.where(place == row + k, lines[k], kept)
                    scale[t] = jnp.where(place == row + k, pivots[k][0], scale[t])
                tiles[t] = kept
            else:
                tiles[t] = tiles[t] - change
    tiles = [t * (1.0 / jnp.sqrt(s)) for t, s in zip(tiles, scale)]
    return jnp.concatenate(tiles, axis=0)[:, BLOCK:]


def inverse_kernel(gram, out, work, lower):
    work[...] = gram[...]
    out[...] = jnp.zeros_like(out)
    count = RANK // BLOCK
    for k in range(count):
        at, end = k * BLOCK, (k + 1) * BLOCK
        small = small_inverse(work[at:end, at:end])
        if k + 1 < count:
            panel = dot(work[end:, at:end], small, 1, 1, HIGHEST)
            lower[end:, at:end] = panel
            work[end:, end:] = work[end:, end:] - dot(panel, panel, 1, 1, HIGHEST)
        if k:
            above = dot(lower[at:end, :at], out[:at, :at], 1, 0, HIGHEST)
            out[at:end, :at] = -dot(small, above, 1, 0, HIGHEST)
        out[at:end, at:end] = small


def factor_inverse(gram):
    return pl.pallas_call(
        inverse_kernel,
        in_specs=[pl.BlockSpec(memory_space=pltpu.VMEM)],
        out_specs=pl.BlockSpec(memory_space=pltpu.VMEM),
        out_shape=jax.ShapeDtypeStruct((RANK, RANK), jnp.float32),
        scratch_shapes=[pltpu.VMEM((RANK, RANK), jnp.float32)] * 2,
        compiler_params=params(16),
        cost_estimate=cost(10_000_000_000, 1_000_000),
    )(gram)


def update_kernel(pos, left, grad, mom, wgt, *refs):
    mine, other = refs[0:5], refs[5:10]
    new_mom, new_wgt, full = refs[10:]
    y, core, i = pos[0], pos[1], pl.program_id(0)
    half = mine[0].shape[1]

    def place(ref, d, first):
        owner = lax.rem(y + NY - d, NY)
        for part in range(2):
            start = ((part * NY + owner) * 2 + first) * half
            full[pl.ds(pl.multiple_of(start, 8), half), :] = ref[part]

    for group, first in ((mine, core), (other, 1 - core)):
        place(group[0], 0, first)
        place(group[1], 1, first)
        place(group[2], 3, first)

        @pl.when(i < 2)
        def _():
            place(group[3], 2, first)

        @pl.when(i >= 2)
        def _():
            place(group[4], 2, first)

    rows = mom.shape[0]
    both = dot_halves(halves(left[...]), halves(full[...]), 1, 1)
    coeff = step_rate * math.sqrt(D / RANK) / math.sqrt(FF)
    keep = 1.0 - step_rate * weight_decay
    summed = mom[...] + grad[...].astype(jnp.float32)
    new_mom[...] = summed - feedback_keep * both[:rows]
    new_wgt[...] = keep * wgt[...] - coeff * both[rows:]


def update(pos, left, gradient, momentum, weight, mine, other):
    rows, cols = momentum.shape
    wide = 2 * cols // NZ
    half = mine[0].shape[1]
    block = pl.BlockSpec((rows, wide), lambda i: (0, i))
    piece = pl.BlockSpec((2, half, RANK), lambda i: (i, 0, 0))
    early = pl.BlockSpec((2, half, RANK), lambda i: (jnp.minimum(i, 1), 0, 0))
    late = pl.BlockSpec((2, half, RANK), lambda i: (jnp.maximum(i - 2, 0), 0, 0))
    pieces = [piece] * 3 + [early, late]
    whole = pl.BlockSpec(left.shape, lambda i: (0, 0))
    return pl.pallas_call(
        update_kernel,
        grid=(NZ // 2,),
        in_specs=[smem(), whole, block, block, block] + pieces + pieces,
        out_specs=[block, block],
        out_shape=[jax.ShapeDtypeStruct(momentum.shape, jnp.float32)] * 2,
        scratch_shapes=[pltpu.VMEM((wide, RANK), jnp.float32)],
        compiler_params=params(48),
        cost_estimate=cost(12 * rows * cols * RANK, rows * cols * 18),
    )(pos, left, gradient, momentum, weight, *mine, *other)


def body(gradient, momentum, weight, basis):
    core, y, x = lax.axis_index("c"), lax.axis_index("y"), lax.axis_index("x")
    pos = jnp.stack([y, core, y * NX + x]).astype(jnp.int32)
    rows, cols = momentum.shape
    shard = basis.shape[0]

    sent = split_columns(gradient, momentum)
    strips = lax.all_to_all(sent, "y", 0, 0)
    basis_z = lax.all_gather(basis, "z", axis=0)
    flat = strips.reshape(NY, NZ * NC * shard, rows)
    near, first, second, third = project(pos, flat, basis_z, swap(basis_z))
    projected = (
        near
        + shift(first, "y", NY, NY - 1)
        + shift(third, "y", NY, 1)
        + shift(second, "y", NY, 2)
    )
    projected = projected + sum(shift(projected, "x", NX, d) for d in range(1, NX))
    projs = [projected] + [shift(projected, "y", NY, d) for d in range(1, NY)]

    mine, other = raw_feedback(pos, strips, projs)
    reduced = scatter_sum(mine + swap(other), "z")
    raw_shard, gram_part = reduced[:shard], reduced[shard:]
    raw = gather(raw_shard, "z", NZ)

    by_y = jnp.stack([gram_part] + [shift(gram_part, "y", NY, d) for d in range(1, NY)])
    by_x = jnp.stack([by_y] + [shift(by_y, "x", NX, d) for d in range(1, NX)])
    by_x = jnp.flip(jnp.concatenate([by_x, by_x], 0), 0)
    by_x = lax.dynamic_slice_in_dim(by_x, NX - 1 - x, NX, 0)
    by_y = jnp.flip(jnp.concatenate([by_x, by_x], 1), 1)
    by_y = lax.dynamic_slice_in_dim(by_y, NY - 1 - y, NY, 1)
    gram_matrix = jnp.swapaxes(by_y, 0, 1).reshape(RANK, RANK)
    inverse = factor_inverse(gram_matrix)

    raw, inverse = lax.optimization_barrier((raw, inverse))
    feedback = dot(raw.reshape(NZ * shard, RANK), inverse, 1, 1)
    squares = jnp.sum(feedback * feedback, axis=0, keepdims=True)
    feedback = feedback.reshape(NZ, shard, RANK)
    ahead = shift(feedback, "y", NY, 1)
    behind = shift(feedback, "y", NY, NY - 1)
    squares = squares + swap(squares)
    squares = jnp.sum(gather(squares, ("y", "x"), NY * NX), axis=0)
    squares, ahead, behind = lax.optimization_barrier((squares, ahead, behind))
    far_low = shift(ahead[: NZ // 2], "y", NY, 1)
    far_high = shift(behind[NZ // 2 :], "y", NY, NY - 1)
    own = [feedback, ahead, behind, far_low, far_high]
    paired = [swap(block) for block in own]
    scales = math.sqrt(FF) / (jnp.sqrt(squares) + epsilon)

    orthonormal = dot(projected, inverse, 1, 1, HIGHEST)
    left = jnp.concatenate([orthonormal, orthonormal * scales], axis=0)
    new_momentum, new_weight = update(
        pos, left, gradient, momentum, weight, own, paired
    )
    new_basis = scales * lax.dynamic_index_in_dim(
        feedback, lax.axis_index("z"), 0, keepdims=False
    )
    return (new_momentum, new_weight, new_basis)


def solution(mesh):
    fine = Mesh(mesh.devices.reshape(NZ, NY, NC, NX), ("z", "y", "c", "x"))
    matrix = P(("z", "y", "c"), "x")
    tall = P(("x", "z", "y", "c"), None)
    return jax.shard_map(
        body,
        mesh=fine,
        in_specs=(matrix, matrix, matrix, tall),
        out_specs=(matrix, matrix, tall),
        check_vma=False,
    )
```

```python
import functools
import math

import jax
import jax.numpy as jnp
from jax import lax
from jax.experimental import pallas as pl
from jax.experimental.pallas import tpu as pltpu
from jax.sharding import Mesh, PartitionSpec as P

D = 8192
FF = 22528
RANK = 256
NZ, NY, NC, NX = 8, 4, 2, 4


epsilon = 1e-06
feedback_keep = 0.05
step_rate = 0.1
weight_decay = 0.1

MIB = 1024 * 1024
HIGHEST = lax.Precision.HIGHEST


def dot(left, right, left_dim, right_dim, precision=lax.Precision.HIGH):
    return lax.dot_general(
        left,
        right,
        (((left_dim,), (right_dim,)), ((), ())),
        precision=precision,
        preferred_element_type=jnp.float32,
    )


def gather(block, axes, count):
    copies = jnp.broadcast_to(block[None], (count,) + block.shape)
    return lax.all_to_all(copies, axes, 0, 0)


def scatter_sum(blocks, axes):
    return jnp.sum(lax.all_to_all(blocks, axes, 0, 0), axis=0)


def swap(block):
    return lax.ppermute(block, "c", [(0, 1), (1, 0)])


def shift(block, axis, size, step):
    return lax.ppermute(block, axis, [(i, (i + step) % size) for i in range(size)])


def halves(value):
    high = value.astype(jnp.bfloat16)
    low = (value - high.astype(jnp.float32)).astype(jnp.bfloat16)
    return high, low


def dot_halves(left, right, left_dim, right_dim):
    def one(a, b):
        return lax.dot_general(
            a,
            b,
            (((left_dim,), (right_dim,)), ((), ())),
            preferred_element_type=jnp.float32,
        )

    (lh, ll), (rh, rl) = left, right
    return one(lh, rh) + (one(lh, rl) + one(ll, rh))


def params(mib):
    return pltpu.CompilerParams(vmem_limit_bytes=mib * MIB)


def cost(flops, size):
    return pl.CostEstimate(flops=flops, bytes_accessed=size, transcendentals=0)


def smem():
    return pl.BlockSpec(memory_space=pltpu.SMEM)


def split_kernel(grad, mom, out, turned):
    turned[...] = (mom[...] + grad[...].astype(jnp.float32)).T
    size = out.shape[2]
    for part in range(out.shape[1]):
        for owner in range(NY):
            start = (part * NY + owner) * size
            out[owner, part] = turned[start : start + size]


def split_columns(gradient, momentum):
    rows, cols = momentum.shape
    steps = 2
    wide = cols // steps
    size = cols // (NZ * NY)
    block = pl.BlockSpec((rows, wide), lambda i: (0, i))
    return pl.pallas_call(
        split_kernel,
        grid=(steps,),
        in_specs=[block, block],
        out_specs=pl.BlockSpec((NY, NZ // steps, size, rows), lambda i: (0, i, 0, 0)),
        out_shape=jax.ShapeDtypeStruct((NY, NZ, size, rows), jnp.float32),
        scratch_shapes=[pltpu.VMEM((wide, rows), jnp.float32)],
        compiler_params=params(60),
        cost_estimate=cost(0, rows * cols * 10),
    )(gradient, momentum)


def project_kernel(pos, strips, mine, other, o0, o1, o2, o3, full):
    y, core = pos[0], pos[1]
    half = mine.shape[1]
    for z in range(NZ):
        start = pl.multiple_of(z * 2 * half + core * half, 8)
        full[pl.ds(start, half), :] = mine[z]
        start = pl.multiple_of(z * 2 * half + (1 - core) * half, 8)
        full[pl.ds(start, half), :] = other[z]
    right = halves(full[...])
    for d, out in enumerate((o0, o1, o2, o3)):
        out[...] = dot_halves(halves(strips[lax.rem(y + NY - d, NY)]), right, 0, 0)


def project(pos, strips, mine, other):
    _, cols, rows = strips.shape
    return pl.pallas_call(
        project_kernel,
        in_specs=[smem()] + [pl.BlockSpec(memory_space=pltpu.VMEM)] * 3,
        out_specs=[pl.BlockSpec(memory_space=pltpu.VMEM)] * NY,
        out_shape=[jax.ShapeDtypeStruct((rows, RANK), jnp.float32)] * NY,
        scratch_shapes=[pltpu.VMEM((cols, RANK), jnp.float32)],
        compiler_params=params(24),
        cost_estimate=cost(6 * NY * rows * cols * RANK, NY * rows * cols * 8),
    )(pos, strips, mine, other)


def feedback_kernel(pos, strips, p0, p1, p2, p3, mine, other, low, high, full, gram):
    y, core = pos[0], pos[1]
    steps, size = strips.shape[1:3]
    half = size // 2
    part = mine.shape[1] - half

    @pl.when(pl.program_id(0) == 0)
    def _():
        proj = jnp.concatenate([p0[...], p1[...], p2[...], p3[...]], axis=0)
        high[...], low[...] = halves(proj)
        gram[...] = dot(proj, proj, 0, 0, HIGHEST)

    mine_at = pl.multiple_of(core * half, 8)
    other_at = pl.multiple_of((1 - core) * half, 8)
    gram_rows = gram[pl.ds(pl.multiple_of(pos[2] * part, 8), part), :]
    for z in range(steps):
        strip = jnp.concatenate(
            [strips[lax.rem(y + NY - d, NY), z] for d in range(NY)], axis=1
        )
        full[...] = dot_halves(halves(strip), (high[...], low[...]), 1, 0)
        mine[z, :half] = full[pl.ds(mine_at, half), :]
        other[z, :half] = full[pl.ds(other_at, half), :]
        mine[z, half:] = gram_rows
        other[z, half:] = gram_rows


def raw_feedback(pos, strips, projs):
    _, _, size, rows = strips.shape
    part = RANK // (NY * NX)
    steps = 2
    strip = pl.BlockSpec((NY, steps, size, rows), lambda z: (0, z, 0, 0))
    proj = pl.BlockSpec((rows, RANK), lambda z: (0, 0))
    out = pl.BlockSpec((steps, size // 2 + part, RANK), lambda z: (z, 0, 0))
    return pl.pallas_call(
        feedback_kernel,
        grid=(NZ // steps,),
        in_specs=[smem(), strip] + [proj] * NY,
        out_specs=[out] * 2,
        out_shape=[jax.ShapeDtypeStruct((NZ, size // 2 + part, RANK), jnp.float32)] * 2,
        scratch_shapes=[
            pltpu.VMEM((NY * rows, RANK), jnp.bfloat16),
            pltpu.VMEM((NY * rows, RANK), jnp.bfloat16),
            pltpu.VMEM((size, RANK), jnp.float32),
            pltpu.VMEM((RANK, RANK), jnp.float32),
        ],
        compiler_params=params(24),
        cost_estimate=cost(6 * NY * rows * NZ * size * RANK, NZ * size * rows * 24),
    )(pos, strips, *projs)


BLOCK = 64
GROUP = 8


def small_inverse(block):
    rows = lax.broadcasted_iota(jnp.int32, (BLOCK, BLOCK), 0)
    cols = lax.broadcasted_iota(jnp.int32, (BLOCK, BLOCK), 1)
    unit = (rows == cols).astype(jnp.float32)
    wide = jnp.concatenate([block, unit], axis=1)
    full = (8, 2 * BLOCK)
    tiles = [wide[8 * t : 8 * t + 8] for t in range(BLOCK // 8)]
    place = lax.broadcasted_iota(jnp.int32, full, 0)
    scale = [jnp.zeros(full, jnp.float32) for _ in tiles]
    for j in range(0, BLOCK, GROUP):
        tile, row = divmod(j, 8)
        cols = {
            t: [jnp.broadcast_to(tiles[t][:, j + k : j + k + 1], full) for k in range(GROUP)]
            for t in range(tile, BLOCK // 8)
        }
        lines = [
            jnp.broadcast_to(tiles[tile][row + k : row + k + 1], full) for k in range(GROUP)
        ]
        heads = [
            [
                jnp.broadcast_to(cols[tile][m][row + k : row + k + 1], full)
                for m in range(k + 1)
            ]
            for k in range(GROUP)
        ]
        pivots = []
        for m in range(GROUP):
            pivot = heads[m][m]
            inverse = 1.0 / pivot
            pivots.append((pivot, inverse))
            for k in range(m + 1, GROUP):
                ratio = heads[k][m] * inverse
                lines[k] = lines[k] - ratio * lines[m]
                for n in range(m + 1, k + 1):
                    heads[k][n] = heads[k][n] - ratio * heads[n][m]
                for t in cols:
                    cols[t][k] = cols[t][k] - ratio * cols[t][m]
        scaled = [line * inverse for line, (_, inverse) in zip(lines, pivots)]
        for t in cols:
            change = cols[t][0] * scaled[0]
            for k in range(1, GROUP):
                change = change + cols[t][k] * scaled[k]
            if t == tile:
                change = jnp.where(place >= row + GROUP, change, 0.0)
                kept = tiles[t] - change
                for k in range(GROUP):
                    kept = jnp.where(place == row + k, lines[k], kept)
                    scale[t] = jnp.where(place == row + k, pivots[k][0], scale[t])
                tiles[t] = kept
            else:
                tiles[t] = tiles[t] - change
    tiles = [t * (1.0 / jnp.sqrt(s)) for t, s in zip(tiles, scale)]
    return jnp.concatenate(tiles, axis=0)[:, BLOCK:]


def inverse_kernel(gram, out, work, lower):
    work[...] = gram[...]
    out[...] = jnp.zeros_like(out)
    count = RANK // BLOCK
    for k in range(count):
        at, end = k * BLOCK, (k + 1) * BLOCK
        small = small_inverse(work[at:end, at:end])
        if k + 1 < count:
            panel = dot(work[end:, at:end], small, 1, 1, HIGHEST)
            lower[end:, at:end] = panel
            work[end:, end:] = work[end:, end:] - dot(panel, panel, 1, 1, HIGHEST)
        if k:
            above = dot(lower[at:end, :at], out[:at, :at], 1, 0, HIGHEST)
            out[at:end, :at] = -dot(small, above, 1, 0, HIGHEST)
        out[at:end, at:end] = small


def factor_inverse(gram):
    return pl.pallas_call(
        inverse_kernel,
        in_specs=[pl.BlockSpec(memory_space=pltpu.VMEM)],
        out_specs=pl.BlockSpec(memory_space=pltpu.VMEM),
        out_shape=jax.ShapeDtypeStruct((RANK, RANK), jnp.float32),
        scratch_shapes=[pltpu.VMEM((RANK, RANK), jnp.float32)] * 2,
        compiler_params=params(16),
        cost_estimate=cost(100_000_000, 1_000_000),
    )(gram)


def update_kernel(pos, left, grad, mom, wgt, *refs):
    new_mom, new_wgt, full, high, low = refs[10:]
    y, core, i = pos[0], pos[1], pl.program_id(0)
    half = refs[0].shape[1]
    near = NZ // 2

    @pl.when(i == 0)
    def _():
        high[...], low[...] = halves(left[...])

    def place(ref, z, part, d, first):
        owner = lax.rem(y + NY - d, NY)
        start = ((part * NY + owner) * 2 + first) * half
        full[pl.ds(pl.multiple_of(start, 8), half), :] = ref[z]

    for group, first in ((refs[:5], core), (refs[5:10], 1 - core)):
        for part in range(2):
            z = 2 * i + part
            place(group[0], z, part, 0, first)
            place(group[1], z, part, 1, first)
            place(group[2], z, part, 3, first)

            @pl.when(z < near)
            def _():
                place(group[3], jnp.minimum(z, near - 1), part, 2, first)

            @pl.when(z >= near)
            def _():
                place(group[4], jnp.maximum(z - near, 0), part, 2, first)

    rows = mom.shape[0]
    both = dot_halves((high[...], low[...]), halves(full[...]), 1, 1)
    coeff = step_rate * math.sqrt(D / RANK) / math.sqrt(FF)
    keep = 1.0 - step_rate * weight_decay
    summed = mom[...] + grad[...].astype(jnp.float32)
    new_mom[...] = summed - feedback_keep * both[:rows]
    new_wgt[...] = keep * wgt[...] - coeff * both[rows:]


def update(pos, left, gradient, momentum, weight, mine, other):
    rows, cols = momentum.shape
    wide = 2 * cols // NZ
    block = pl.BlockSpec((rows, wide), lambda i: (0, i))
    whole = pl.BlockSpec(memory_space=pltpu.VMEM)
    return pl.pallas_call(
        update_kernel,
        grid=(NZ // 2,),
        in_specs=[smem(), whole, block, block, block] + [whole] * 10,
        out_specs=[block, block],
        out_shape=[jax.ShapeDtypeStruct(momentum.shape, jnp.float32)] * 2,
        scratch_shapes=[
            pltpu.VMEM((wide, RANK), jnp.float32),
            pltpu.VMEM(left.shape, jnp.bfloat16),
            pltpu.VMEM(left.shape, jnp.bfloat16),
        ],
        compiler_params=params(48),
        cost_estimate=cost(12 * rows * cols * RANK, rows * cols * 18),
    )(pos, left, gradient, momentum, weight, *mine, *other)


def body(gradient, momentum, weight, basis):
    core, y, x = lax.axis_index("c"), lax.axis_index("y"), lax.axis_index("x")
    pos = jnp.stack([y, core, y * NX + x]).astype(jnp.int32)
    rows, cols = momentum.shape
    shard = basis.shape[0]

    sent = split_columns(gradient, momentum)
    strips = lax.all_to_all(sent, "y", 0, 0)
    basis_z = lax.all_gather(basis, "z", axis=0)
    flat = strips.reshape(NY, NZ * NC * shard, rows)
    near, first, second, third = project(pos, flat, basis_z, swap(basis_z))
    projected = (
        near
        + shift(first, "y", NY, NY - 1)
        + shift(third, "y", NY, 1)
        + shift(second, "y", NY, 2)
    )
    projected = projected + sum(shift(projected, "x", NX, d) for d in range(1, NX))
    projs = [projected] + [shift(projected, "y", NY, d) for d in range(1, NY)]

    mine, other = raw_feedback(pos, strips, projs)
    reduced = scatter_sum(mine + swap(other), "z")
    raw_shard, gram_part = reduced[:shard], reduced[shard:]
    raw = gather(raw_shard, "z", NZ)

    by_y = jnp.stack([gram_part] + [shift(gram_part, "y", NY, d) for d in range(1, NY)])
    by_x = jnp.stack([by_y] + [shift(by_y, "x", NX, d) for d in range(1, NX)])
    by_x = jnp.flip(jnp.concatenate([by_x, by_x], 0), 0)
    by_x = lax.dynamic_slice_in_dim(by_x, NX - 1 - x, NX, 0)
    by_y = jnp.flip(jnp.concatenate([by_x, by_x], 1), 1)
    by_y = lax.dynamic_slice_in_dim(by_y, NY - 1 - y, NY, 1)
    gram_matrix = jnp.swapaxes(by_y, 0, 1).reshape(RANK, RANK)
    inverse = factor_inverse(gram_matrix)

    raw, inverse = lax.optimization_barrier((raw, inverse))
    feedback = dot(raw.reshape(NZ * shard, RANK), inverse, 1, 1)
    squares = jnp.sum(feedback * feedback, axis=0, keepdims=True)
    feedback = feedback.reshape(NZ, shard, RANK)
    ahead = shift(feedback, "y", NY, 1)
    behind = shift(feedback, "y", NY, NY - 1)
    squares = squares + swap(squares)
    squares = jnp.sum(gather(squares, ("y", "x"), NY * NX), axis=0)
    squares, ahead, behind = lax.optimization_barrier((squares, ahead, behind))
    far_low = shift(ahead[: NZ // 2], "y", NY, 1)
    far_high = shift(behind[NZ // 2 :], "y", NY, NY - 1)
    own = [feedback, ahead, behind, far_low, far_high]
    paired = [swap(block) for block in own]
    scales = math.sqrt(FF) / (jnp.sqrt(squares) + epsilon)

    orthonormal = dot(projected, inverse, 1, 1, HIGHEST)
    left = jnp.concatenate([orthonormal, orthonormal * scales], axis=0)
    new_momentum, new_weight = update(
        pos, left, gradient, momentum, weight, own, paired
    )
    new_basis = scales * lax.dynamic_index_in_dim(
        feedback, lax.axis_index("z"), 0, keepdims=False
    )
    return (new_momentum, new_weight, new_basis)


def solution(mesh):
    fine = Mesh(mesh.devices.reshape(NZ, NY, NC, NX), ("z", "y", "c", "x"))
    matrix = P(("z", "y", "c"), "x")
    tall = P(("x", "z", "y", "c"), None)
    return jax.shard_map(
        body,
        mesh=fine,
        in_specs=(matrix, matrix, matrix, tall),
        out_specs=(matrix, matrix, tall),
        check_vma=False,
    )
```

```python
import functools
import math

import jax
import jax.numpy as jnp
from jax import lax
from jax.experimental import pallas as pl
from jax.experimental.pallas import tpu as pltpu
from jax.sharding import Mesh, PartitionSpec as P

D = 8192
FF = 22528
RANK = 256
NZ, NY, NC, NX = 8, 4, 2, 4


epsilon = 1e-06
feedback_keep = 0.05
step_rate = 0.1
weight_decay = 0.1

MIB = 1024 * 1024
HIGHEST = lax.Precision.HIGHEST


def dot(left, right, left_dim, right_dim, precision=lax.Precision.HIGH):
    return lax.dot_general(
        left,
        right,
        (((left_dim,), (right_dim,)), ((), ())),
        precision=precision,
        preferred_element_type=jnp.float32,
    )


def gather(block, axes, count):
    copies = jnp.broadcast_to(block[None], (count,) + block.shape)
    return lax.all_to_all(copies, axes, 0, 0)


def swap(block):
    return lax.ppermute(block, "c", [(0, 1), (1, 0)])


def shift(block, axis, size, step):
    return lax.ppermute(block, axis, [(i, (i + step) % size) for i in range(size)])


def halves(value):
    high = value.astype(jnp.bfloat16)
    low = (value - high.astype(jnp.float32)).astype(jnp.bfloat16)
    return high, low


def dot_halves(left, right, left_dim, right_dim):
    def one(a, b):
        return lax.dot_general(
            a,
            b,
            (((left_dim,), (right_dim,)), ((), ())),
            preferred_element_type=jnp.float32,
        )

    (lh, ll), (rh, rl) = left, right
    return one(lh, rh) + (one(lh, rl) + one(ll, rh))


def params(mib):
    return pltpu.CompilerParams(vmem_limit_bytes=mib * MIB)


def cost(flops, size):
    return pl.CostEstimate(flops=flops, bytes_accessed=size, transcendentals=0)


def smem():
    return pl.BlockSpec(memory_space=pltpu.SMEM)


def split_kernel(grad, mom, out, turned):
    turned[...] = (mom[...] + grad[...].astype(jnp.float32)).T
    size = out.shape[2]
    for part in range(out.shape[1]):
        for owner in range(NY):
            start = (part * NY + owner) * size
            out[owner, part] = turned[start : start + size]


def split_columns(gradient, momentum):
    rows, cols = momentum.shape
    steps = 2
    wide = cols // steps
    size = cols // (NZ * NY)
    block = pl.BlockSpec((rows, wide), lambda i: (0, i))
    return pl.pallas_call(
        split_kernel,
        grid=(steps,),
        in_specs=[block, block],
        out_specs=pl.BlockSpec((NY, NZ // steps, size, rows), lambda i: (0, i, 0, 0)),
        out_shape=jax.ShapeDtypeStruct((NY, NZ, size, rows), jnp.float32),
        scratch_shapes=[pltpu.VMEM((wide, rows), jnp.float32)],
        compiler_params=params(60),
        cost_estimate=cost(0, rows * cols * 10),
    )(gradient, momentum)


def project_kernel(pos, strips, mine, other, o0, o1, o2, o3, full):
    y, core = pos[0], pos[1]
    half = mine.shape[1]
    for z in range(NZ):
        start = pl.multiple_of(z * 2 * half + core * half, 8)
        full[pl.ds(start, half), :] = mine[z]
        start = pl.multiple_of(z * 2 * half + (1 - core) * half, 8)
        full[pl.ds(start, half), :] = other[z]
    right = halves(full[...])
    for d, out in enumerate((o0, o1, o2, o3)):
        out[...] = dot_halves(halves(strips[lax.rem(y + NY - d, NY)]), right, 0, 0)


def project(pos, strips, mine, other):
    _, cols, rows = strips.shape
    return pl.pallas_call(
        project_kernel,
        in_specs=[smem()] + [pl.BlockSpec(memory_space=pltpu.VMEM)] * 3,
        out_specs=[pl.BlockSpec(memory_space=pltpu.VMEM)] * NY,
        out_shape=[jax.ShapeDtypeStruct((rows, RANK), jnp.float32)] * NY,
        scratch_shapes=[pltpu.VMEM((cols, RANK), jnp.float32)],
        compiler_params=params(24),
        cost_estimate=cost(6 * NY * rows * cols * RANK, NY * rows * cols * 8),
    )(pos, strips, mine, other)


def feedback_kernel(pos, strips, p0, p1, p2, p3, mine, other, low, high, full, gram):
    y, core = pos[0], pos[1]
    steps, size = strips.shape[1:3]
    half = size // 2
    part = mine.shape[1] - half

    @pl.when(pl.program_id(0) == 0)
    def _():
        proj = jnp.concatenate([p0[...], p1[...], p2[...], p3[...]], axis=0)
        high[...], low[...] = halves(proj)
        gram[...] = dot(proj, proj, 0, 0, HIGHEST)

    mine_at = pl.multiple_of(core * half, 8)
    other_at = pl.multiple_of((1 - core) * half, 8)
    gram_rows = gram[pl.ds(pl.multiple_of(pos[2] * part, 8), part), :]
    for z in range(steps):
        strip = jnp.concatenate(
            [strips[lax.rem(y + NY - d, NY), z] for d in range(NY)], axis=1
        )
        full[...] = dot_halves(halves(strip), (high[...], low[...]), 1, 0)
        mine[z, :half] = full[pl.ds(mine_at, half), :]
        other[z, :half] = full[pl.ds(other_at, half), :]
        mine[z, half:] = gram_rows
        other[z, half:] = gram_rows


def raw_feedback(pos, strips, projs):
    _, _, size, rows = strips.shape
    part = RANK // (NY * NX)
    steps = 4
    strip = pl.BlockSpec((NY, steps, size, rows), lambda z: (0, z, 0, 0))
    proj = pl.BlockSpec((rows, RANK), lambda z: (0, 0))
    out = pl.BlockSpec((steps, size // 2 + part, RANK), lambda z: (z, 0, 0))
    return pl.pallas_call(
        feedback_kernel,
        grid=(NZ // steps,),
        in_specs=[smem(), strip] + [proj] * NY,
        out_specs=[out] * 2,
        out_shape=[jax.ShapeDtypeStruct((NZ, size // 2 + part, RANK), jnp.float32)] * 2,
        scratch_shapes=[
            pltpu.VMEM((NY * rows, RANK), jnp.bfloat16),
            pltpu.VMEM((NY * rows, RANK), jnp.bfloat16),
            pltpu.VMEM((size, RANK), jnp.float32),
            pltpu.VMEM((RANK, RANK), jnp.float32),
        ],
        compiler_params=params(24),
        cost_estimate=cost(6 * NY * rows * NZ * size * RANK, NZ * size * rows * 24),
    )(pos, strips, *projs)


def share_kernel(parts, copies, gram):
    total = parts[0]
    for k in range(1, parts.shape[0]):
        total = total + parts[k]
    shard = copies.shape[1]
    for k in range(copies.shape[0]):
        copies[k] = total[:shard]
    gram[...] = total[shard:]


def share(parts, shard):
    count, rows, _ = parts.shape
    return pl.pallas_call(
        share_kernel,
        in_specs=[pl.BlockSpec(memory_space=pltpu.VMEM)],
        out_specs=[pl.BlockSpec(memory_space=pltpu.VMEM)] * 2,
        out_shape=[
            jax.ShapeDtypeStruct((count, shard, RANK), jnp.float32),
            jax.ShapeDtypeStruct((rows - shard, RANK), jnp.float32),
        ],
        compiler_params=params(8),
        cost_estimate=cost(count * rows * RANK, 2 * count * rows * RANK * 4),
    )(parts)


BLOCK = 64
GROUP = 8


def small_inverse(block):
    rows = lax.broadcasted_iota(jnp.int32, (BLOCK, BLOCK), 0)
    cols = lax.broadcasted_iota(jnp.int32, (BLOCK, BLOCK), 1)
    unit = (rows == cols).astype(jnp.float32)
    wide = jnp.concatenate([block, unit], axis=1)
    full = (8, 2 * BLOCK)
    tiles = [wide[8 * t : 8 * t + 8] for t in range(BLOCK // 8)]
    place = lax.broadcasted_iota(jnp.int32, full, 0)
    scale = [jnp.zeros(full, jnp.float32) for _ in tiles]
    for j in range(0, BLOCK, GROUP):
        tile, row = divmod(j, 8)
        cols = {
            t: [jnp.broadcast_to(tiles[t][:, j + k : j + k + 1], full) for k in range(GROUP)]
            for t in range(tile, BLOCK // 8)
        }
        lines = [
            jnp.broadcast_to(tiles[tile][row + k : row + k + 1], full) for k in range(GROUP)
        ]
        heads = [
            [
                jnp.broadcast_to(cols[tile][m][row + k : row + k + 1], full)
                for m in range(k + 1)
            ]
            for k in range(GROUP)
        ]
        pivots = []
        for m in range(GROUP):
            pivot = heads[m][m]
            inverse = 1.0 / pivot
            pivots.append((pivot, inverse))
            for k in range(m + 1, GROUP):
                ratio = heads[k][m] * inverse
                lines[k] = lines[k] - ratio * lines[m]
                for n in range(m + 1, k + 1):
                    heads[k][n] = heads[k][n] - ratio * heads[n][m]
                for t in cols:
                    cols[t][k] = cols[t][k] - ratio * cols[t][m]
        scaled = [line * inverse for line, (_, inverse) in zip(lines, pivots)]
        for t in cols:
            change = cols[t][0] * scaled[0]
            for k in range(1, GROUP):
                change = change + cols[t][k] * scaled[k]
            if t == tile:
                change = jnp.where(place >= row + GROUP, change, 0.0)
                kept = tiles[t] - change
                for k in range(GROUP):
                    kept = jnp.where(place == row + k, lines[k], kept)
                    scale[t] = jnp.where(place == row + k, pivots[k][0], scale[t])
                tiles[t] = kept
            else:
                tiles[t] = tiles[t] - change
    tiles = [t * (1.0 / jnp.sqrt(s)) for t, s in zip(tiles, scale)]
    return jnp.concatenate(tiles, axis=0)[:, BLOCK:]


def inverse_kernel(gram, out, work, lower):
    work[...] = gram[...]
    out[...] = jnp.zeros_like(out)
    count = RANK // BLOCK
    for k in range(count):
        at, end = k * BLOCK, (k + 1) * BLOCK
        small = small_inverse(work[at:end, at:end])
        if k + 1 < count:
            panel = dot(work[end:, at:end], small, 1, 1, HIGHEST)
            lower[end:, at:end] = panel
            work[end:, end:] = work[end:, end:] - dot(panel, panel, 1, 1, HIGHEST)
        if k:
            above = dot(lower[at:end, :at], out[:at, :at], 1, 0, HIGHEST)
            out[at:end, :at] = -dot(small, above, 1, 0, HIGHEST)
        out[at:end, at:end] = small


def factor_inverse(gram):
    return pl.pallas_call(
        inverse_kernel,
        in_specs=[pl.BlockSpec(memory_space=pltpu.VMEM)],
        out_specs=pl.BlockSpec(memory_space=pltpu.VMEM),
        out_shape=jax.ShapeDtypeStruct((RANK, RANK), jnp.float32),
        scratch_shapes=[pltpu.VMEM((RANK, RANK), jnp.float32)] * 2,
        compiler_params=params(16),
        cost_estimate=cost(100_000_000, 1_000_000),
    )(gram)


def update_kernel(pos, left, grad, mom, wgt, *refs):
    new_mom, new_wgt, full, high, low = refs[10:]
    y, core, i = pos[0], pos[1], pl.program_id(0)
    half = refs[0].shape[1]
    near = NZ // 2

    @pl.when(i == 0)
    def _():
        high[...], low[...] = halves(left[...])

    def place(ref, z, part, d, first):
        owner = lax.rem(y + NY - d, NY)
        start = ((part * NY + owner) * 2 + first) * half
        full[pl.ds(pl.multiple_of(start, 8), half), :] = ref[z]

    for group, first in ((refs[:5], core), (refs[5:10], 1 - core)):
        for part in range(2):
            z = 2 * i + part
            place(group[0], z, part, 0, first)
            place(group[1], z, part, 1, first)
            place(group[2], z, part, 3, first)

            @pl.when(z < near)
            def _():
                place(group[3], jnp.minimum(z, near - 1), part, 2, first)

            @pl.when(z >= near)
            def _():
                place(group[4], jnp.maximum(z - near, 0), part, 2, first)

    rows = mom.shape[0]
    both = dot_halves((high[...], low[...]), halves(full[...]), 1, 1)
    coeff = step_rate * math.sqrt(D / RANK) / math.sqrt(FF)
    keep = 1.0 - step_rate * weight_decay
    summed = mom[...] + grad[...].astype(jnp.float32)
    new_mom[...] = summed - feedback_keep * both[:rows]
    new_wgt[...] = keep * wgt[...] - coeff * both[rows:]


def update(pos, left, gradient, momentum, weight, mine, other):
    rows, cols = momentum.shape
    wide = 2 * cols // NZ
    block = pl.BlockSpec((rows, wide), lambda i: (0, i))
    whole = pl.BlockSpec(memory_space=pltpu.VMEM)
    return pl.pallas_call(
        update_kernel,
        grid=(NZ // 2,),
        in_specs=[smem(), whole, block, block, block] + [whole] * 10,
        out_specs=[block, block],
        out_shape=[jax.ShapeDtypeStruct(momentum.shape, jnp.float32)] * 2,
        scratch_shapes=[
            pltpu.VMEM((wide, RANK), jnp.float32),
            pltpu.VMEM(left.shape, jnp.bfloat16),
            pltpu.VMEM(left.shape, jnp.bfloat16),
        ],
        compiler_params=params(48),
        cost_estimate=cost(12 * rows * cols * RANK, rows * cols * 18),
    )(pos, left, gradient, momentum, weight, *mine, *other)


def body(gradient, momentum, weight, basis):
    core, y, x = lax.axis_index("c"), lax.axis_index("y"), lax.axis_index("x")
    pos = jnp.stack([y, core, y * NX + x]).astype(jnp.int32)
    rows, cols = momentum.shape
    shard = basis.shape[0]

    sent = split_columns(gradient, momentum)
    strips = lax.all_to_all(sent, "y", 0, 0)
    basis_z = lax.all_gather(basis, "z", axis=0)
    flat = strips.reshape(NY, NZ * NC * shard, rows)
    near, first, second, third = project(pos, flat, basis_z, swap(basis_z))
    projected = (
        near
        + shift(first, "y", NY, NY - 1)
        + shift(third, "y", NY, 1)
        + shift(second, "y", NY, 2)
    )
    projected = projected + sum(shift(projected, "x", NX, d) for d in range(1, NX))
    projs = [projected] + [shift(projected, "y", NY, d) for d in range(1, NY)]

    mine, other = raw_feedback(pos, strips, projs)
    parts = lax.all_to_all(mine + swap(other), "z", 0, 0)
    copies, gram_part = share(parts, shard)
    raw = lax.all_to_all(copies, "z", 0, 0)

    by_y = jnp.stack([gram_part] + [shift(gram_part, "y", NY, d) for d in range(1, NY)])
    by_x = jnp.stack([by_y] + [shift(by_y, "x", NX, d) for d in range(1, NX)])
    by_x = jnp.flip(jnp.concatenate([by_x, by_x], 0), 0)
    by_x = lax.dynamic_slice_in_dim(by_x, NX - 1 - x, NX, 0)
    by_y = jnp.flip(jnp.concatenate([by_x, by_x], 1), 1)
    by_y = lax.dynamic_slice_in_dim(by_y, NY - 1 - y, NY, 1)
    gram_matrix = jnp.swapaxes(by_y, 0, 1).reshape(RANK, RANK)
    inverse = factor_inverse(gram_matrix)

    raw, inverse = lax.optimization_barrier((raw, inverse))
    feedback = dot(raw.reshape(NZ * shard, RANK), inverse, 1, 1)
    squares = jnp.sum(feedback * feedback, axis=0, keepdims=True)
    feedback = feedback.reshape(NZ, shard, RANK)
    ahead = shift(feedback, "y", NY, 1)
    behind = shift(feedback, "y", NY, NY - 1)
    squares = squares + swap(squares)
    squares = jnp.sum(gather(squares, ("y", "x"), NY * NX), axis=0)
    squares, ahead, behind = lax.optimization_barrier((squares, ahead, behind))
    far_low = shift(ahead[: NZ // 2], "y", NY, 1)
    far_high = shift(behind[NZ // 2 :], "y", NY, NY - 1)
    own = [feedback, ahead, behind, far_low, far_high]
    paired = [swap(block) for block in own]
    scales = math.sqrt(FF) / (jnp.sqrt(squares) + epsilon)

    orthonormal = dot(projected, inverse, 1, 1, HIGHEST)
    left = jnp.concatenate([orthonormal, orthonormal * scales], axis=0)
    new_momentum, new_weight = update(
        pos, left, gradient, momentum, weight, own, paired
    )
    new_basis = scales * lax.dynamic_index_in_dim(
        feedback, lax.axis_index("z"), 0, keepdims=False
    )
    return (new_momentum, new_weight, new_basis)


def solution(mesh):
    fine = Mesh(mesh.devices.reshape(NZ, NY, NC, NX), ("z", "y", "c", "x"))
    matrix = P(("z", "y", "c"), "x")
    tall = P(("x", "z", "y", "c"), None)
    return jax.shard_map(
        body,
        mesh=fine,
        in_specs=(matrix, matrix, matrix, tall),
        out_specs=(matrix, matrix, tall),
        check_vma=False,
    )
```
